32 devices in a mesh: row: 8 (over y, x, core), col: 4 (over z).
Axes of the slice: x: 2, y: 2, z: 4, core: 2. Of those that a mesh axis runs over, the one named last changes fastest.
Arguments:
- leaf_basis: float32 [64, 64, 256], P(('row', 'col')), may hold values from -0.375 to 0.375
- child_transfer: float32 [64, 4096], P(('row', 'col')), may hold values from -0.5 to 2
- top_transfer: float32 [32, 5, 4096], P(('row', 'col')), may hold values from -0.5 to 2, as said below
- vectors: bfloat16 [16384, 1024], P(('row', 'col')), may hold values from -6 to 6
- near_blocks: bfloat16 [320, 256, 256], P(('row', 'col')), may hold values from -0.375 to 0.375
- near_rows: int32 [320], P(('row', 'col')), may hold values from 0 to 63, as said below
- near_cols: int32 [320], P(('row', 'col')), may hold values from 0 to 63, as said below
- near_counts: int32 [32], P(('row', 'col')), may hold values from 2 to 10, as said below
- coupling: float32 [480, 4096], P(('row', 'col')), may hold values from -0.75 to 0.75
- coupling_rows: int32 [480], P(('row', 'col')), may hold values from 0 to 63, as said below
- coupling_cols: int32 [480], P(('row', 'col')), may hold values from 0 to 63, as said below
- block_counts: int32 [32, 2], P(('row', 'col')), may hold values from 0 to 10, as said below
Outputs:
- ortho_basis: float32 [64, 64, 256], P(('row', 'col'))
- child_new: float32 [64, 4096], P(('row', 'col'))
- top_new: float32 [32, 5, 4096], P(('row', 'col'))
- coupling_new: float32 [480, 4096], P(('row', 'col'))
- product: bfloat16 [16384, 1024], P(('row', 'col'))
The draws below stay inside these ranges and needn't reach their ends.
Inputs may be any that keep to these rules, and one draw needn't show every extreme that they name: `near_rows`: block i holds rows i * 10 to i * 10 + 9. Its first near_counts[i] slots are live, in no particular order, no pair twice; a live slot's row leaf is one of leaves 2 * i and 2 * i + 1, and its column leaf lies at most 2 leaves from it; every such leaf's pair with itself is live. The other slots hold leaf 2 * i in both entries. `near_cols`: see near_rows. `near_counts`: the bound 10 is reached by some block in every draw. `coupling_rows`: block i holds rows i * 15 to i * 15 + 14: first 10 slots of leaf pairs, then 5 slots of pairs of clusters of level one. In each part the first block_counts[i, level] slots are live, in no particular order, no pair twice; a live slot's row cluster belongs to block i (leaves 2 * i and 2 * i + 1, or cluster i), and its column cluster of the same level lies more than 2 and at most 5 clusters from it. The other slots hold the block's first cluster of that level in both entries. `coupling_cols`: see coupling_rows. `block_counts`: column 0 is at most 10, column 1 at most 5; both bounds are reached by some block in every draw. top_transfer[n, a] is the same for all n with the same n // 2 ** a.
All inputs are finite; a program needn't handle non-finite values.
Results may differ from the reference program's by a relative error of at most 0.0095.
Values may be sent and summed in bfloat16 or wider, within the bound.
A program may use at most 64 MiB of HBM per device.

```python
import math
import jax
import jax.numpy as jnp
from jax import lax

LEAF = 256
RANK = 64
NVEC = 1024
LEAVES_DEV = 2
NEAR_REACH = 2
FAR_MAX = 5
CAND = 5
NODES = 32
NLEAF = 64
NPTS = 16384
NEARCAP = 10
BCAP = 15
TOP = 5


def transfer_matrices(key, count):
    diagonal_key, spread_key = jax.random.split(key)
    diagonal = jax.random.uniform(diagonal_key, (count, RANK), jnp.float32, 0.8, 1.2)
    spread = 0.3 / math.sqrt(RANK) * jnp.clip(jax.random.normal(spread_key, (count, RANK, RANK), jnp.float32), -4.0, 4.0)
    identity = jnp.eye(RANK, dtype=jnp.float32)
    return (identity[None] * diagonal[:, None, :] + spread).reshape(count, RANK * RANK)


def draw_child_transfer(key, part):
    return transfer_matrices(jax.random.fold_in(key, 7), NLEAF)


def draw_top_transfer(key, part):
    levels = []
    for level_index in range(TOP):
        group_step = 2 ** level_index
        fresh = transfer_matrices(jax.random.fold_in(key, 100 + level_index), NODES // group_step)
        levels.append(jnp.repeat(fresh, group_step, axis=0))
    return jnp.stack(levels, axis=1)


def compact(key, chosen, row_ids, columns, per_block):
    width_slots = per_block * chosen.shape[1]
    chosen = chosen.reshape(NODES, width_slots)
    row_ids = row_ids.reshape(NODES, width_slots)
    columns = columns.reshape(NODES, width_slots)
    jitter = jax.random.randint(key, (NODES, width_slots), 0, 64)
    sort_key = (1 - chosen.astype(jnp.int32)) * 4096 + jitter * 64 + jnp.arange(width_slots, dtype=jnp.int32)[None, :]
    ranking = jnp.argsort(sort_key, axis=1, stable=True)
    chosen = jnp.take_along_axis(chosen, ranking, axis=1)
    row_ids = jnp.take_along_axis(row_ids, ranking, axis=1)
    columns = jnp.take_along_axis(columns, ranking, axis=1)
    own_first = (jnp.arange(NODES, dtype=jnp.int32) * per_block)[:, None]
    row_ids = jnp.where(chosen, row_ids, own_first)
    columns = jnp.where(chosen, columns, own_first)
    return (row_ids, columns, jnp.sum(chosen.astype(jnp.int32), axis=1))


def near_lists(key):
    base_key = jax.random.fold_in(key, 31)
    chosen_key = jax.random.fold_in(base_key, 1)
    jitter_key = jax.random.fold_in(base_key, 2)
    full_block = jax.random.randint(jax.random.fold_in(base_key, 3), (), 1, NODES - 1)
    cluster = jnp.arange(NLEAF, dtype=jnp.int32)
    spread = jnp.arange(-NEAR_REACH, NEAR_REACH + 1, dtype=jnp.int32)
    columns = cluster[:, None] + spread[None, :]
    inside = (columns >= 0) & (columns < NLEAF)
    chosen = jax.random.randint(chosen_key, columns.shape, 0, 4) > 0
    chosen = chosen | (spread[None, :] == 0) | (cluster // LEAVES_DEV == full_block)[:, None]
    chosen = chosen & inside
    row_ids = jnp.broadcast_to(cluster[:, None], columns.shape)
    return compact(jitter_key, chosen, row_ids, columns, LEAVES_DEV)


def coupling_level(key, total, per_block, full_block):
    chosen_key, jitter_key = jax.random.split(key)
    cluster = jnp.arange(total, dtype=jnp.int32)
    even_steps = jnp.array([-4, -3, 3, 4, 5], jnp.int32)
    odd_steps = jnp.array([-5, -4, -3, 3, 4], jnp.int32)
    step_table = jnp.where((cluster % 2 == 0)[:, None], even_steps[None, :], odd_steps[None, :])
    columns = cluster[:, None] + step_table
    inside = (columns >= 0) & (columns < total)
    chosen = jax.random.randint(chosen_key, columns.shape, 0, 4) > 0
    chosen = (chosen | (cluster // per_block == full_block)[:, None]) & inside
    row_ids = jnp.broadcast_to(cluster[:, None], columns.shape)
    return compact(jitter_key, chosen, row_ids, columns, per_block)


def coupling_lists(key):
    base_key = jax.random.fold_in(key, 53)
    full_block = jax.random.randint(jax.random.fold_in(base_key, 1), (), FAR_MAX, NODES - FAR_MAX)
    leaf_rows, leaf_cols, leaf_counts = coupling_level(jax.random.fold_in(base_key, 2), NLEAF, LEAVES_DEV, full_block)
    node_rows, node_cols, node_counts = coupling_level(jax.random.fold_in(base_key, 3), NODES, 1, full_block)
    row_ids = jnp.concatenate([leaf_rows, node_rows], axis=1).reshape(-1)
    columns = jnp.concatenate([leaf_cols, node_cols], axis=1).reshape(-1)
    return (row_ids, columns, jnp.stack([leaf_counts, node_counts], axis=1))


def draw_near_rows(key, part):
    return near_lists(key)[0].reshape(-1)


def draw_near_cols(key, part):
    return near_lists(key)[1].reshape(-1)


def draw_near_counts(key, part):
    return near_lists(key)[2]


def draw_coupling_rows(key, part):
    return coupling_lists(key)[0]


def draw_coupling_cols(key, part):
    return coupling_lists(key)[1]


def draw_block_counts(key, part):
    return coupling_lists(key)[2]


def steps_of(own_key, dims, shards, smallest, largest):
    def one(dim, parts):
        heights = jax.random.uniform(jax.random.fold_in(jax.random.fold_in(own_key, 6), dim), (parts,), jnp.float32, smallest / len(shards), largest / len(shards))
        return jnp.repeat(jnp.exp(heights), dims[dim] // parts).reshape((-1,) + (1,) * (len(dims) - dim - 1))

    factor_of = one(*shards[0])
    for cut in shards[1:]:
        factor_of = factor_of * one(*cut)
    return factor_of


def centred(key, extent, scale, bound, cuts=(), held_as=jnp.bfloat16):
    values = jax.random.normal(key, extent, jnp.float32) * scale
    if len(cuts) > 0:
        values = steps_of(key, extent, cuts, -0.22, 0.18) * values
    return jnp.clip(values, min=-bound, max=bound).astype(held_as)


def setup_inputs(seed: int = 0) -> dict:
    arg_keys = jax.random.split(jax.random.key(seed), 13)
    leaf_basis = centred(arg_keys[0], (NLEAF, RANK, LEAF), LEAF ** -0.5, 0.375, ((0, 32),), jnp.float32)
    child_transfer = draw_child_transfer(jax.random.fold_in(arg_keys[12], 71), 0)
    top_transfer = draw_top_transfer(jax.random.fold_in(arg_keys[12], 71), 0)
    vectors = centred(arg_keys[3], (NPTS, NVEC), 1.0, 6.0, ((0, 32),))
    near_blocks = centred(arg_keys[4], (NODES * NEARCAP, LEAF, LEAF), LEAF ** -0.5, 0.375, ((0, 32),))
    near_rows = draw_near_rows(jax.random.fold_in(arg_keys[12], 71), 0)
    near_cols = draw_near_cols(jax.random.fold_in(arg_keys[12], 71), 0)
    near_counts = draw_near_counts(jax.random.fold_in(arg_keys[12], 71), 0)
    coupling = centred(arg_keys[8], (NODES * BCAP, RANK * RANK), RANK ** -0.5, 0.75, ((0, 32),), jnp.float32)
    coupling_rows = draw_coupling_rows(jax.random.fold_in(arg_keys[12], 71), 0)
    coupling_cols = draw_coupling_cols(jax.random.fold_in(arg_keys[12], 71), 0)
    block_counts = draw_block_counts(jax.random.fold_in(arg_keys[12], 71), 0)
    return dict(leaf_basis=leaf_basis, child_transfer=child_transfer, top_transfer=top_transfer, vectors=vectors, near_blocks=near_blocks, near_rows=near_rows, near_cols=near_cols, near_counts=near_counts, coupling=coupling, coupling_rows=coupling_rows, coupling_cols=coupling_cols, block_counts=block_counts)


HIGHEST_PRECISION = lax.Precision.HIGHEST

def lower_solve(lower_factor, right_side):
    return jax.vmap(lambda matrix, column: jax.scipy.linalg.solve_triangular(matrix, column, lower=True))(lower_factor, right_side)

def lift_level(lower_factor, transfer):
    lifted = jnp.einsum('nji,njk->nik', lower_factor, transfer, precision=HIGHEST_PRECISION)
    gram_terms = jnp.einsum('nji,njk->nik', lifted, lifted, precision=HIGHEST_PRECISION)
    return (lifted, gram_terms)

def reproject(lower_factor, lifted):
    return jnp.swapaxes(lower_solve(lower_factor, jnp.swapaxes(lifted, 1, 2)), 1, 2)

def reference(leaf_basis, child_transfer, top_transfer, vectors, near_blocks, near_rows, near_cols, near_counts, coupling, coupling_rows, coupling_cols, block_counts):
    leaf_gram = jnp.einsum('lkp,ljp->lkj', leaf_basis, leaf_basis, precision=HIGHEST_PRECISION)
    leaf_lower = jnp.linalg.cholesky(leaf_gram)
    ortho_basis = lower_solve(leaf_lower, leaf_basis)
    lifted, gram_terms = lift_level(leaf_lower, child_transfer.reshape(NLEAF, RANK, RANK))
    node_gram = gram_terms[0::2] + gram_terms[1::2]
    node_lower = jnp.linalg.cholesky(node_gram)
    child_new = reproject(jnp.repeat(node_lower, LEAVES_DEV, axis=0), lifted)
    lower_now = node_lower
    top_levels = []
    for level_index in range(TOP):
        group_step = 2 ** level_index
        transfer_now = top_transfer[0::group_step, level_index].reshape(-1, RANK, RANK)
        up_lifted, up_terms = lift_level(lower_now, transfer_now)
        lower_now = jnp.linalg.cholesky(up_terms[0::2] + up_terms[1::2])
        fresh = reproject(jnp.repeat(lower_now, 2, axis=0), up_lifted)
        top_levels.append(jnp.repeat(fresh, group_step, axis=0).reshape(NODES, RANK * RANK))
    top_new = jnp.stack(top_levels, axis=1)
    ortho_low = ortho_basis.astype(jnp.bfloat16)
    ortho_blocks = ortho_low.reshape(NODES, LEAVES_DEV, RANK, LEAF)
    vector_blocks = vectors.reshape(NODES, LEAVES_DEV, LEAF, NVEC)
    child_blocks = child_new.reshape(NODES, LEAVES_DEV, RANK, RANK)

    def coefficients(pieces):
        ortho_here, vector_here, child_here = pieces
        leaf_coeff = jnp.einsum('lkp,lpv->lkv', ortho_here.astype(jnp.float32), vector_here.astype(jnp.float32), precision=HIGHEST_PRECISION)
        node_coeff = jnp.einsum('lij,liv->jv', child_here, leaf_coeff, precision=HIGHEST_PRECISION)
        return jnp.concatenate([leaf_coeff, node_coeff[None]], axis=0).astype(jnp.bfloat16)
    coeff_low = lax.map(coefficients, (ortho_blocks, vector_blocks, child_blocks))
    factor_all = jnp.concatenate([leaf_lower.reshape(NODES, LEAVES_DEV, RANK, RANK), node_lower[:, None]], axis=1)
    coeff_pad = jnp.pad(coeff_low, ((FAR_MAX, FAR_MAX), (0, 0), (0, 0), (0, 0)))
    factor_pad = jnp.pad(factor_all, ((FAR_MAX, FAR_MAX), (0, 0), (0, 0), (0, 0)))
    vector_pad = jnp.pad(vectors.reshape(NLEAF, LEAF, NVEC), ((NEAR_REACH, NEAR_REACH), (0, 0), (0, 0)))
    node_count = LEAVES_DEV + 1

    def per_block(pieces):
        device, blocks_here, nrow_here, ncol_here, ncount_here, slots_here, crow_here, ccol_here, counts_here, ortho_here, child_here, factor_here = pieces
        slot_index = jnp.arange(BCAP, dtype=jnp.int32)
        level_split = CAND * LEAVES_DEV
        upper_level = slot_index >= level_split
        active = jnp.where(upper_level, slot_index - level_split < counts_here[1], slot_index < counts_here[0])
        node_span = jnp.where(upper_level, 1, LEAVES_DEV).astype(jnp.int32)
        stack_base = jnp.where(upper_level, LEAVES_DEV, 0).astype(jnp.int32)
        row_local = jnp.where(active, crow_here - device * node_span + stack_base, stack_base).astype(jnp.int32)
        source = (ccol_here // node_span).astype(jnp.int32)
        position = jnp.where(active, (source - device + FAR_MAX) * node_count + ccol_here - source * node_span + stack_base, FAR_MAX * node_count + stack_base).astype(jnp.int32)
        factor_window = lax.dynamic_slice_in_dim(factor_pad, device, 2 * FAR_MAX + 1, 0).reshape(-1, RANK, RANK)
        coeff_window = lax.dynamic_slice_in_dim(coeff_pad, device, 2 * FAR_MAX + 1, 0).reshape(-1, RANK, NVEC)
        col_lower = jnp.take(factor_window, position, axis=0)
        row_lower = jnp.take(factor_here, row_local, axis=0)
        left_half = jnp.einsum('bji,bjk->bik', row_lower, slots_here, precision=HIGHEST_PRECISION)
        recompressed = jnp.einsum('bik,bkj->bij', left_half, col_lower, precision=HIGHEST_PRECISION)
        recompressed = jnp.where(active[:, None, None], recompressed, 0.0)
        coupling_low = recompressed.astype(jnp.bfloat16)
        gathered = jnp.take(coeff_window, position, axis=0)
        far_terms = jnp.einsum('bij,bjv->biv', coupling_low.astype(jnp.float32), gathered.astype(jnp.float32), precision=HIGHEST_PRECISION)
        row_onehot = (row_local[:, None] == jnp.arange(node_count, dtype=jnp.int32)[None, :]).astype(jnp.float32)
        collected = jnp.einsum('bn,biv->niv', row_onehot, far_terms, precision=HIGHEST_PRECISION)
        descended = (collected[:LEAVES_DEV] + jnp.einsum('lij,jv->liv', child_here, collected[LEAVES_DEV], precision=HIGHEST_PRECISION)).astype(jnp.bfloat16)
        far_part = jnp.einsum('lkp,lkv->lpv', ortho_here.astype(jnp.float32), descended.astype(jnp.float32), precision=HIGHEST_PRECISION)
        near_active = jnp.arange(NEARCAP, dtype=jnp.int32) < ncount_here
        near_row = jnp.where(near_active, nrow_here - device * LEAVES_DEV, 0).astype(jnp.int32)
        near_col = jnp.where(near_active, ncol_here - device * LEAVES_DEV + NEAR_REACH, NEAR_REACH).astype(jnp.int32)
        window = lax.dynamic_slice_in_dim(vector_pad, device * LEAVES_DEV, LEAVES_DEV + 2 * NEAR_REACH, 0)
        sources = jnp.take(window, near_col, axis=0)
        near_terms = jnp.einsum('bij,bjv->biv', blocks_here.astype(jnp.float32), sources.astype(jnp.float32), precision=HIGHEST_PRECISION)
        near_terms = jnp.where(near_active[:, None, None], near_terms, 0.0)
        near_onehot = (near_row[:, None] == jnp.arange(LEAVES_DEV, dtype=jnp.int32)[None, :]).astype(jnp.float32)
        near_sum = jnp.einsum('br,biv->riv', near_onehot, near_terms, precision=HIGHEST_PRECISION)
        result = (near_sum + far_part).astype(jnp.bfloat16).reshape(LEAVES_DEV * LEAF, NVEC)
        return (recompressed.reshape(BCAP, RANK * RANK), result)
    block_inputs = (jnp.arange(NODES, dtype=jnp.int32), near_blocks.reshape(NODES, NEARCAP, LEAF, LEAF), near_rows.reshape(NODES, NEARCAP), near_cols.reshape(NODES, NEARCAP), near_counts, coupling.reshape(NODES, BCAP, RANK, RANK), coupling_rows.reshape(NODES, BCAP), coupling_cols.reshape(NODES, BCAP), block_counts, ortho_blocks, child_blocks, factor_all)
    coupling_parts, product_parts = lax.map(per_block, block_inputs)
    coupling_new = coupling_parts.reshape(NODES * BCAP, RANK * RANK)
    product = product_parts.reshape(NPTS, NVEC)
    return (ortho_basis, child_new.reshape(NLEAF, RANK * RANK), top_new, coupling_new, product)
```

```python
import jax
import jax.numpy as jnp
from jax import lax
from jax.experimental import pallas as pl
from jax.experimental.pallas import tpu as pltpu
from jax.sharding import PartitionSpec as P

AXES = ("row", "col")
HI = lax.Precision.HIGHEST
F32 = jnp.float32
BF16 = jnp.bfloat16
MESH = pl.DeviceIdType.MESH
PANEL = 8
SENDS = (
    (2, 1, 2, 2),
    (-2, 1, 2, 4),
    (3, 2, 2, 6),
    (-3, 0, 2, 8),
    (1, 1, 1, 0),
    (-1, 2, 1, 1),
    (5, 0, 1, 12),
    (-5, 0, 1, 13),
    (4, 0, 1, 10),
    (-4, 0, 1, 11),
)
SLOTS = 14


def mm(a, b, ca=1, cb=0, precision=HI):
    return lax.dot_general(
        a, b, (((ca,), (cb,)), ((), ())), precision=precision, preferred_element_type=F32
    )


def factor(grams):
    n = grams[0].shape[0]
    row = lax.broadcasted_iota(jnp.int32, (n, n), 0)
    col = lax.broadcasted_iota(jnp.int32, (n, n), 1)
    eye = jnp.where(row == col, 1.0, 0.0).astype(F32)
    wide = 2 * n
    top_row = lax.broadcasted_iota(jnp.int32, (PANEL, wide), 0)
    rest_row = lax.broadcasted_iota(jnp.int32, (n - PANEL, wide), 0) + PANEL
    start = tuple(jnp.concatenate([g, eye], axis=1) for g in grams)

    def panel(p, mats):
        live = rest_row < n - PANEL * p
        out = []
        for m in mats:
            top, rest = m[:PANEL], m[PANEL:]
            ctop = [jnp.broadcast_to(top[:, k : k + 1], (PANEL, wide)) for k in range(PANEL)]
            crest = [jnp.broadcast_to(rest[:, k : k + 1], (n - PANEL, wide)) for k in range(PANEL)]
            for j in range(PANEL):
                r = lax.rsqrt(ctop[j][j : j + 1])
                nj = top[j : j + 1] * r
                lt = ctop[j] * r
                lr = jnp.where(live, crest[j] * r, 0.0)
                top = jnp.where(
                    top_row > j, top - lt * nj, jnp.where(top_row == j, nj, top)
                )
                rest = rest - lr * nj
                for k in range(j + 1, PANEL):
                    lk = lt[k : k + 1]
                    ctop[k] = ctop[k] - lt * lk
                    crest[k] = crest[k] - lr * lk
            out.append(pltpu.roll(jnp.concatenate([rest, top], axis=0), wide - PANEL, 1))
        return tuple(out)

    done = lax.fori_loop(0, n // PANEL, panel, start)
    return [(jnp.where(col >= row, m[:, n:], 0.0), m[:, :n]) for m in done]


def tree_kernel(
    shape,
    levels,
    basis_ref,
    child_ref,
    upper_ref,
    vec_ref,
    ortho_ref,
    child_new_ref,
    top_new_ref,
    lower_ref,
    window_ref,
    table_ref,
    x_ref,
    stack_ref,
    term_ref,
    got_ref,
    x_sem,
    send_sem,
    recv_sem,
):
    rows, cols = shape
    total = rows * cols
    me = lax.axis_index("row") * cols + lax.axis_index("col")

    def place(distance):
        other = lax.rem(me + distance + total, total)
        return (other // cols, lax.rem(other, cols))

    def partner(level):
        step = 2**level
        other = me + step * (1 - 2 * lax.rem(me // step, 2))
        return (other // cols, lax.rem(other, cols))

    load = pltpu.make_async_copy(vec_ref, x_ref, x_sem)
    load.start()
    barrier = pltpu.get_barrier_semaphore()
    for send in SENDS:
        pl.semaphore_signal(barrier, inc=1, device_id=place(send[0]), device_id_type=MESH)
    for level in range(levels):
        pl.semaphore_signal(barrier, inc=1, device_id=partner(level), device_id_type=MESH)
    pl.semaphore_wait(barrier, len(SENDS) + levels)

    copies = []

    def send(src, dst, where):
        at = len(copies)
        copy = pltpu.make_async_remote_copy(
            src_ref=src,
            dst_ref=dst,
            send_sem=send_sem.at[at],
            recv_sem=recv_sem.at[at],
            device_id=where,
            device_id_type=MESH,
        )
        copy.start()
        copies.append(copy)
        return copy

    send(vec_ref, window_ref.at[0], place(1))
    send(vec_ref, window_ref.at[1], place(-1))

    leaf_count, rank, points = basis_ref.shape
    nvec = x_ref.shape[1]
    pad = jnp.zeros((rank, rank), BF16)

    def pack(entry, coeff, lower_t):
        stack_ref[entry, :, :nvec] = coeff.astype(BF16)
        stack_ref[entry, :, nvec:] = jnp.concatenate([lower_t.astype(BF16), pad], axis=1)

    leaves = factor([mm(basis_ref[l], basis_ref[l], 1, 1) for l in range(leaf_count)])
    ortho = [mm(leaves[l][1], basis_ref[l]) for l in range(leaf_count)]
    lifted = [mm(leaves[l][0], child_ref[l]) for l in range(leaf_count)]
    node_gram = mm(lifted[0], lifted[0], 0, 0) + mm(lifted[1], lifted[1], 0, 0)
    for l in range(leaf_count):
        ortho_ref[l] = ortho[l]
        lower_ref[l] = leaves[l][0]
    load.wait()
    coeffs = []
    for l in range(leaf_count):
        coeff = mm(
            ortho[l].astype(BF16), x_ref[l * points : (l + 1) * points, :], precision=None
        )
        coeffs.append(coeff)
        pack(1 + l, coeff, leaves[l][0])
    for distance, first, count, slot in SENDS:
        if first == 1 or (first == 2 and count == 1):
            send(
                stack_ref.at[pl.ds(first, count)], table_ref.at[pl.ds(slot, count)], place(distance)
            )
    ((lower_t, inverse),) = factor([node_gram])
    lower_ref[leaf_count] = lower_t
    fresh = [mm(lifted[l], inverse, 1, 1) for l in range(leaf_count)]
    for l in range(leaf_count):
        child_new_ref[l] = fresh[l]
    node_coeff = mm(fresh[0], coeffs[0], 0, 0) + mm(fresh[1], coeffs[1], 0, 0)
    pack(0, node_coeff, lower_t)
    pack(3, node_coeff, lower_t)
    for distance, first, count, slot in SENDS:
        if not (first == 1 or (first == 2 and count == 1)):
            send(
                stack_ref.at[pl.ds(first, count)], table_ref.at[pl.ds(slot, count)], place(distance)
            )
    for level in range(levels):
        up = mm(lower_t, upper_ref[level])
        term = mm(up, up, 0, 0)
        term_ref[level] = term
        copy = send(term_ref.at[level], got_ref.at[level], partner(level))
        copy.wait_recv()
        ((lower_t, inverse),) = factor([term + got_ref[level]])
        top_new_ref[level] = mm(up, inverse, 1, 1)
    for at, copy in enumerate(copies):
        copy.wait_send()
        if at < 2 + len(SENDS):
            copy.wait_recv()


def apply_kernel(
    shape,
    blocks_ref,
    window_ref,
    vec_ref,
    ortho_ref,
    child_ref,
    lower_ref,
    table_ref,
    coupling_ref,
    near_rows,
    near_cols,
    near_counts,
    far_rows,
    far_cols,
    far_counts,
    coupling_new_ref,
    product_ref,
    near_ref,
    far_ref,
    desc_ref,
):
    me = lax.axis_index("row") * shape[1] + lax.axis_index("col")
    slots, points, _ = blocks_ref.shape
    leaf_count, rank, _ = ortho_ref.shape
    nvec = vec_ref.shape[1]
    reach = window_ref.shape[1] // points
    near_ref[...] = jnp.zeros_like(near_ref)
    for b in range(slots):

        @pl.when(b < near_counts[0])
        def _():
            r = near_rows[b] - me * leaf_count
            c = near_cols[b] - me * leaf_count + reach
            near_ref[
                pl.ds(pl.multiple_of(r * points, points), points),
                pl.ds(pl.multiple_of(c * points, points), points),
            ] = blocks_ref[b]

    far_ref[...] = jnp.zeros_like(far_ref)
    split = coupling_ref.shape[0] * leaf_count // (leaf_count + 1)
    for b in range(coupling_ref.shape[0]):
        upper = b >= split
        if upper:
            active = b - split < far_counts[0, 1]
            row = leaf_count
            delta = far_cols[b] - me
            slot = jnp.where(
                delta == -3,
                7,
                jnp.where(
                    delta == 3,
                    8,
                    jnp.where(
                        delta == -4, 10, jnp.where(delta == 4, 11, jnp.where(delta == -5, 12, 13))
                    ),
                ),
            )
        else:
            active = b < far_counts[0, 0]
            row = jnp.where(active, far_rows[b] - me * leaf_count, 0)
            delta = far_cols[b] - me * leaf_count
            odd = lax.rem(far_cols[b], 2)
            slot = jnp.where(
                delta < -4,
                6,
                jnp.where(
                    delta < -2,
                    2 + odd,
                    jnp.where(
                        delta < 0, 0, jnp.where(delta < 4, 1, jnp.where(delta < 6, 4 + odd, 9))
                    ),
                ),
            )
        slot = jnp.where(active, slot, 0)
        item = table_ref[slot]
        half = mm(lower_ref[row], coupling_ref[b])
        new = mm(half, item[:, nvec : nvec + rank].astype(F32), 1, 1)
        new = jnp.where(active, new, 0.0)
        coupling_new_ref[b] = new
        low = new.astype(BF16)
        term = mm(low, item[:, :nvec], precision=None)
        far_ref[row] = far_ref[row] + term
    for l in range(leaf_count):
        desc_ref[l] = (far_ref[l] + mm(child_ref[l], far_ref[leaf_count])).astype(BF16)
    tile = 256

    @pl.loop(0, nvec // tile)
    def _(step):
        at = pl.ds(pl.multiple_of(step * tile, tile), tile)
        side = reach * points
        acc = mm(near_ref[:, :side], window_ref[0, :, at], precision=None)
        acc = acc + mm(
            near_ref[:, side : side + leaf_count * points], vec_ref[:, at], precision=None
        )
        acc = acc + mm(
            near_ref[:, side + leaf_count * points :], window_ref[1, :, at], precision=None
        )
        for l in range(leaf_count):
            far = mm(ortho_ref[l].astype(BF16), desc_ref[l, :, at], 0, 0, precision=None)
            product_ref[l * points : (l + 1) * points, at] = (
                acc[l * points : (l + 1) * points] + far
            ).astype(BF16)


def body(
    shape,
    leaf_basis,
    child_transfer,
    top_transfer,
    vectors,
    near_blocks,
    near_rows,
    near_cols,
    near_counts,
    coupling,
    coupling_rows,
    coupling_cols,
    block_counts,
):
    leaf_count, rank, points = leaf_basis.shape
    nvec = vectors.shape[1]
    levels = top_transfer.shape[1]
    square = (rank, rank)
    vmem = pl.BlockSpec(memory_space=pltpu.VMEM)
    smem = pl.BlockSpec(memory_space=pltpu.SMEM)
    hbm = pl.BlockSpec(memory_space=pl.ANY)
    copies = 2 + len(SENDS) + levels
    held = nvec + 2 * rank

    def tree(*refs):
        tree_kernel(shape, levels, *refs)

    ortho, child_new, top_new, lowers, window, table = pl.pallas_call(
        tree,
        name="tree",
        out_shape=(
            jax.ShapeDtypeStruct(leaf_basis.shape, F32),
            jax.ShapeDtypeStruct((leaf_count,) + square, F32),
            jax.ShapeDtypeStruct((levels,) + square, F32),
            jax.ShapeDtypeStruct((leaf_count + 1,) + square, F32),
            jax.ShapeDtypeStruct((2,) + vectors.shape, BF16),
            jax.ShapeDtypeStruct((SLOTS, rank, held), BF16),
        ),
        in_specs=[vmem, vmem, vmem, hbm],
        out_specs=(vmem, vmem, vmem, vmem, hbm, hbm),
        scratch_shapes=[
            pltpu.VMEM(vectors.shape, BF16),
            pltpu.VMEM((4, rank, held), BF16),
            pltpu.VMEM((levels,) + square, F32),
            pltpu.VMEM((levels,) + square, F32),
            pltpu.SemaphoreType.DMA,
            pltpu.SemaphoreType.DMA((copies,)),
            pltpu.SemaphoreType.DMA((copies,)),
        ],
        compiler_params=pltpu.CompilerParams(
            collective_id=0, has_side_effects=True, vmem_limit_bytes=32 * 1024 * 1024
        ),
    )(
        leaf_basis,
        child_transfer.reshape((leaf_count,) + square),
        top_transfer.reshape((levels,) + square),
        vectors,
    )

    def apply(*refs):
        apply_kernel(shape, *refs)

    coupling_new, product = pl.pallas_call(
        apply,
        name="apply",
        out_shape=(
            jax.ShapeDtypeStruct((coupling.shape[0],) + square, F32),
            jax.ShapeDtypeStruct(vectors.shape, BF16),
        ),
        in_specs=[vmem] * 8 + [smem] * 6,
        out_specs=(vmem, vmem),
        scratch_shapes=[
            pltpu.VMEM((leaf_count * points, 3 * leaf_count * points), BF16),
            pltpu.VMEM((leaf_count + 1, rank, nvec), F32),
            pltpu.VMEM((leaf_count, rank, nvec), BF16),
        ],
        compiler_params=pltpu.CompilerParams(vmem_limit_bytes=48 * 1024 * 1024),
    )(
        near_blocks,
        window,
        vectors,
        ortho,
        child_new,
        lowers,
        table,
        coupling.reshape((-1,) + square),
        near_rows,
        near_cols,
        near_counts,
        coupling_rows,
        coupling_cols,
        block_counts,
    )
    return (
        ortho,
        child_new.reshape(leaf_count, -1),
        top_new.reshape(1, levels, -1),
        coupling_new.reshape(coupling.shape),
        product,
    )


def solution(mesh):
    shape = (mesh.shape["row"], mesh.shape["col"])
    ranks = (3, 2, 3, 2, 3, 1, 1, 1, 2, 1, 1, 2)

    def run(*args):
        return body(shape, *args)

    def spec(rank):
        return P(AXES, *([None] * (rank - 1)))

    return jax.shard_map(
        run,
        mesh=mesh,
        in_specs=tuple(spec(rank) for rank in ranks),
        out_specs=tuple(spec(rank) for rank in (3, 2, 3, 2, 2)),
        check_vma=False,
    )
```

```python
import jax
import jax.numpy as jnp
from jax import lax
from jax.experimental import pallas as pl
from jax.experimental.pallas import tpu as pltpu
from jax.sharding import PartitionSpec as P

AXES = ("row", "col")
HI = lax.Precision.HIGHEST
F32 = jnp.float32
BF16 = jnp.bfloat16
MESH = pl.DeviceIdType.MESH
PANEL = 8
SENDS = (
    (2, 1, 2, 2),
    (-2, 1, 2, 4),
    (3, 2, 2, 6),
    (-3, 0, 2, 8),
    (1, 1, 1, 0),
    (-1, 2, 1, 1),
    (5, 0, 1, 12),
    (-5, 0, 1, 13),
    (4, 0, 1, 10),
    (-4, 0, 1, 11),
)
SLOTS = 14
RELAY_COLS = 4
RELAY_SLOTS = 38
NEEDED = {1: (0, 1), 2: (0, 2), 3: (1, 2), 4: (2, 1), 5: (2, 1)}
NEEDED_BACK = {1: (1, 1), 2: (0, 2), 3: (0, 3), 4: (2, 1), 5: (2, 1)}


def mm(a, b, ca=1, cb=0, precision=HI):
    return lax.dot_general(
        a, b, (((ca,), (cb,)), ((), ())), precision=precision, preferred_element_type=F32
    )


def factor(grams):
    n = grams[0].shape[0]
    row = lax.broadcasted_iota(jnp.int32, (n, n), 0)
    col = lax.broadcasted_iota(jnp.int32, (n, n), 1)
    eye = jnp.where(row == col, 1.0, 0.0).astype(F32)
    wide = 2 * n
    top_row = lax.broadcasted_iota(jnp.int32, (PANEL, wide), 0)
    rest_row = lax.broadcasted_iota(jnp.int32, (n - PANEL, wide), 0) + PANEL
    start = tuple(jnp.concatenate([g, eye], axis=1) for g in grams)

    def panel(p, mats):
        live = rest_row < n - PANEL * p
        out = []
        for m in mats:
            top, rest = m[:PANEL], m[PANEL:]
            ctop = [jnp.broadcast_to(top[:, k : k + 1], (PANEL, wide)) for k in range(PANEL)]
            crest = [jnp.broadcast_to(rest[:, k : k + 1], (n - PANEL, wide)) for k in range(PANEL)]
            for j in range(PANEL):
                r = lax.rsqrt(ctop[j][j : j + 1])
                nj = top[j : j + 1] * r
                lt = ctop[j] * r
                lr = jnp.where(live, crest[j] * r, 0.0)
                top = jnp.where(
                    top_row > j, top - lt * nj, jnp.where(top_row == j, nj, top)
                )
                rest = rest - lr * nj
                for k in range(j + 1, PANEL):
                    lk = lt[k : k + 1]
                    ctop[k] = ctop[k] - lt * lk
                    crest[k] = crest[k] - lr * lk
            out.append(pltpu.roll(jnp.concatenate([rest, top], axis=0), wide - PANEL, 1))
        return tuple(out)

    done = lax.fori_loop(0, n // PANEL, panel, start)
    return [(jnp.where(col >= row, m[:, n:], 0.0), m[:, :n]) for m in done]


def tree_kernel(
    shape,
    levels,
    basis_ref,
    child_ref,
    upper_ref,
    vec_ref,
    ortho_ref,
    child_new_ref,
    top_new_ref,
    lower_ref,
    window_ref,
    table_ref,
    x_ref,
    stack_ref,
    term_ref,
    got_ref,
    x_sem,
    send_sem,
    recv_sem,
):
    rows, cols = shape
    total = rows * cols
    me = lax.axis_index("row") * cols + lax.axis_index("col")

    def place(distance):
        other = lax.rem(me + distance + total, total)
        return (other // cols, lax.rem(other, cols))

    def partner(level):
        step = 2**level
        other = me + step * (1 - 2 * lax.rem(me // step, 2))
        return (other // cols, lax.rem(other, cols))

    relay = cols == RELAY_COLS
    here, z = me // cols, lax.rem(me, cols)

    def beside(rows_off, cols_off):
        return (lax.rem(here + rows_off + rows, rows), lax.rem(z + cols_off + cols, cols))

    load = pltpu.make_async_copy(vec_ref, x_ref, x_sem)
    load.start()
    barrier = pltpu.get_barrier_semaphore()
    if relay:
        peers = [place(1), place(-1)]
        peers += [beside(0, 1), beside(0, -1)]
        peers += [beside(1, 0), beside(-1, 0), beside(2, 0), beside(-2, 0)]
    else:
        peers = [place(send[0]) for send in SENDS]
    peers += [partner(level) for level in range(levels)]
    for peer in peers:
        pl.semaphore_signal(barrier, inc=1, device_id=peer, device_id_type=MESH)
    pl.semaphore_wait(barrier, len(peers))

    def remote(at, src, dst, where):
        return pltpu.make_async_remote_copy(
            src_ref=src,
            dst_ref=dst,
            send_sem=send_sem.at[at],
            recv_sem=recv_sem.at[at],
            device_id=where,
            device_id_type=MESH,
        )

    leaf_count, rank, points = basis_ref.shape
    nvec = x_ref.shape[1]
    half = vec_ref.shape[0] // 2

    def vector_copy(part, side):
        at = pl.ds(part * half, half)
        return remote(
            2 * part + side, vec_ref.at[at], window_ref.at[side, at], place(1 - 2 * side)
        )

    vector_copies = [vector_copy(part, side) for part in range(2) for side in range(2)]
    vector_copies[0].start()
    vector_copies[1].start()

    def direct_copy(index):
        distance, first, count, slot = SENDS[index]
        return remote(
            4 + index,
            stack_ref.at[pl.ds(first, count)],
            table_ref.at[pl.ds(slot, count)],
            place(distance),
        )

    def own_row(source, first=0, count=3):
        return table_ref.at[pl.ds((cols + source) * 3 + first, count)]

    def hop(stage, side):
        way = 1 - 2 * side
        at = own_row(z - way * stage)
        return remote(4 + 2 * stage + side, at, at, beside(0, way))

    def hop_in(stage, side):
        way = 1 - 2 * side
        at = own_row(z - way * (stage + 1))
        return remote(4 + 2 * stage + side, at, at, beside(0, way))

    def sends_hop(stage, side):
        if side == 0:
            return jnp.logical_and(z >= stage, z < cols - 1)
        return jnp.logical_and(z < cols - stage, z > 0)

    def gets_hop(stage, side):
        return z > stage if side == 0 else z < cols - 1 - stage

    def row_copies(column, source):
        found = []
        ahead, back = cols + column - source, cols - column + source
        if ahead in NEEDED:
            first, count = NEEDED[ahead]
            found.append(
                remote(
                    10 + source,
                    own_row(source, first, count),
                    table_ref.at[pl.ds(source * 3 + first, count)],
                    beside(1, 0),
                )
            )
        if back in NEEDED_BACK:
            first, count = NEEDED_BACK[back]
            found.append(
                remote(
                    14 + source,
                    own_row(source, first, count),
                    table_ref.at[pl.ds((2 * cols + source) * 3 + first, count)],
                    beside(-1, 0),
                )
            )
        if column == 0 and source == cols - 1:
            found.append(
                remote(
                    18, own_row(source, 2, 1), table_ref.at[pl.ds(9 * cols, 1)], beside(2, 0)
                )
            )
        if column == cols - 1 and source == 0:
            found.append(
                remote(
                    19, own_row(source, 2, 1), table_ref.at[pl.ds(9 * cols + 1, 1)], beside(-2, 0)
                )
            )
        return found

    def start_rows(away):
        for column in range(cols):
            sources = sorted({column - away, column + away})

            @pl.when(z == column)
            def _():
                for source in sources:
                    if 0 <= source < cols:
                        for copy in row_copies(column, source):
                            copy.start()

    def start_hops(stage):
        for side in range(2):

            @pl.when(sends_hop(stage, side))
            def _():
                hop(stage, side).start()

    def take_hops(stage):
        for side in range(2):

            @pl.when(gets_hop(stage, side))
            def _():
                hop_in(stage, side).wait_recv()

    pad = jnp.zeros((rank, rank), BF16)

    def pack(entry, coeff, lower_t):
        stack_ref[entry, :, :nvec] = coeff.astype(BF16)
        stack_ref[entry, :, nvec:] = jnp.concatenate([lower_t.astype(BF16), pad], axis=1)

    leaves = factor([mm(basis_ref[l], basis_ref[l], 1, 1) for l in range(leaf_count)])
    ortho = [mm(leaves[l][1], basis_ref[l]) for l in range(leaf_count)]
    lifted = [mm(leaves[l][0], child_ref[l]) for l in range(leaf_count)]
    node_gram = mm(lifted[0], lifted[0], 0, 0) + mm(lifted[1], lifted[1], 0, 0)
    for l in range(leaf_count):
        ortho_ref[l] = ortho[l]
        lower_ref[l] = leaves[l][0]
    load.wait()
    coeffs = []
    for l in range(leaf_count):
        coeff = mm(
            ortho[l].astype(BF16), x_ref[l * points : (l + 1) * points, :], precision=None
        )
        coeffs.append(coeff)
        pack(1 + l, coeff, leaves[l][0])
    ((lower_t, inverse),) = factor([node_gram])
    lower_ref[leaf_count] = lower_t
    fresh = [mm(lifted[l], inverse, 1, 1) for l in range(leaf_count)]
    for l in range(leaf_count):
        child_new_ref[l] = fresh[l]
    node_coeff = mm(fresh[0], coeffs[0], 0, 0) + mm(fresh[1], coeffs[1], 0, 0)
    pack(0, node_coeff, lower_t)
    pack(3, node_coeff, lower_t)
    if relay:
        keep = pltpu.make_async_copy(stack_ref.at[pl.ds(1, 3)], own_row(z), x_sem)
        keep.start()
        keep.wait()
        start_hops(0)
        start_rows(0)
    else:
        for index in range(len(SENDS)):
            direct_copy(index).start()
    vector_copies[2].start()
    vector_copies[3].start()
    exchanges = []
    for level in range(levels):
        up = mm(lower_t, upper_ref[level])
        term = mm(up, up, 0, 0)
        term_ref[level] = term
        copy = remote(20 + level, term_ref.at[level], got_ref.at[level], partner(level))
        copy.start()
        exchanges.append(copy)
        if relay and level in (2, 4):
            take_hops(level // 2 - 1)
            start_hops(level // 2)
            start_rows(level // 2)
        copy.wait_recv()
        ((lower_t, inverse),) = factor([term + got_ref[level]])
        top_new_ref[level] = mm(up, inverse, 1, 1)
    if relay:
        for stage in range(cols - 1):
            if 2 * stage + 2 >= levels:
                take_hops(stage)
                if stage + 1 < cols - 1:
                    start_hops(stage + 1)
                start_rows(stage + 1)
        for stage in range(cols - 1):
            for side in range(2):

                @pl.when(sends_hop(stage, side))
                def _():
                    hop(stage, side).wait_send()

        for column in range(cols):

            @pl.when(z == column)
            def _():
                for source in range(cols):
                    for copy in row_copies(column, source):
                        copy.wait_send()
                for source in range(cols):
                    for copy in row_copies(column, source):
                        copy.wait_recv()

    else:
        for index in range(len(SENDS)):
            direct_copy(index).wait()
    for copy in exchanges:
        copy.wait_send()
    for copy in vector_copies:
        copy.wait()


def apply_kernel(
    shape,
    blocks_ref,
    window_ref,
    vec_ref,
    ortho_ref,
    child_ref,
    lower_ref,
    table_ref,
    coupling_ref,
    near_rows,
    near_cols,
    near_counts,
    far_rows,
    far_cols,
    far_counts,
    coupling_new_ref,
    product_ref,
    near_ref,
    far_ref,
    desc_ref,
):
    me = lax.axis_index("row") * shape[1] + lax.axis_index("col")
    slots, points, _ = blocks_ref.shape
    leaf_count, rank, _ = ortho_ref.shape
    nvec = vec_ref.shape[1]
    reach = window_ref.shape[1] // points
    near_ref[...] = jnp.zeros_like(near_ref)
    for b in range(slots):

        @pl.when(b < near_counts[0])
        def _():
            r = near_rows[b] - me * leaf_count
            c = near_cols[b] - me * leaf_count + reach
            near_ref[
                pl.ds(pl.multiple_of(r * points, points), points),
                pl.ds(pl.multiple_of(c * points, points), points),
            ] = blocks_ref[b]

    far_ref[...] = jnp.zeros_like(far_ref)
    split = coupling_ref.shape[0] * leaf_count // (leaf_count + 1)
    for b in range(coupling_ref.shape[0]):
        upper = b >= split
        if upper:
            active = b - split < far_counts[0, 1]
            row = leaf_count
            delta = far_cols[b] - me
            slot = jnp.where(
                delta == -3,
                7,
                jnp.where(
                    delta == 3,
                    8,
                    jnp.where(
                        delta == -4, 10, jnp.where(delta == 4, 11, jnp.where(delta == -5, 12, 13))
                    ),
                ),
            )
        else:
            active = b < far_counts[0, 0]
            row = jnp.where(active, far_rows[b] - me * leaf_count, 0)
            delta = far_cols[b] - me * leaf_count
            odd = lax.rem(far_cols[b], 2)
            slot = jnp.where(
                delta < -4,
                6,
                jnp.where(
                    delta < -2,
                    2 + odd,
                    jnp.where(
                        delta < 0, 0, jnp.where(delta < 4, 1, jnp.where(delta < 6, 4 + odd, 9))
                    ),
                ),
            )
        if shape[1] == RELAY_COLS:
            cols = shape[1]
            span = 1 if upper else leaf_count
            entry = leaf_count if upper else lax.rem(far_cols[b], leaf_count)
            source = jnp.where(active, far_cols[b] // span, me)
            apart = source // cols - me // cols
            slot = ((apart + 1) * cols + lax.rem(source, cols)) * 3 + entry
            slot = jnp.where(apart < -1, 9 * cols, jnp.where(apart > 1, 9 * cols + 1, slot))
        else:
            slot = jnp.where(active, slot, 0)
        item = table_ref[slot]
        half = mm(lower_ref[row], coupling_ref[b])
        new = mm(half, item[:, nvec : nvec + rank].astype(F32), 1, 1)
        new = jnp.where(active, new, 0.0)
        coupling_new_ref[b] = new
        low = new.astype(BF16)
        term = mm(low, item[:, :nvec], precision=None)
        far_ref[row] = far_ref[row] + term
    for l in range(leaf_count):
        desc_ref[l] = (far_ref[l] + mm(child_ref[l], far_ref[leaf_count])).astype(BF16)
    tile = 256

    @pl.loop(0, nvec // tile)
    def _(step):
        at = pl.ds(pl.multiple_of(step * tile, tile), tile)
        side = reach * points
        acc = mm(near_ref[:, :side], window_ref[0, :, at], precision=None)
        acc = acc + mm(
            near_ref[:, side : side + leaf_count * points], vec_ref[:, at], precision=None
        )
        acc = acc + mm(
            near_ref[:, side + leaf_count * points :], window_ref[1, :, at], precision=None
        )
        for l in range(leaf_count):
            far = mm(ortho_ref[l].astype(BF16), desc_ref[l, :, at], 0, 0, precision=None)
            product_ref[l * points : (l + 1) * points, at] = (
                acc[l * points : (l + 1) * points] + far
            ).astype(BF16)


def body(
    shape,
    leaf_basis,
    child_transfer,
    top_transfer,
    vectors,
    near_blocks,
    near_rows,
    near_cols,
    near_counts,
    coupling,
    coupling_rows,
    coupling_cols,
    block_counts,
):
    leaf_count, rank, points = leaf_basis.shape
    nvec = vectors.shape[1]
    levels = top_transfer.shape[1]
    square = (rank, rank)
    vmem = pl.BlockSpec(memory_space=pltpu.VMEM)
    smem = pl.BlockSpec(memory_space=pltpu.SMEM)
    hbm = pl.BlockSpec(memory_space=pl.ANY)
    copies = 20 + levels
    slots = RELAY_SLOTS if shape[1] == RELAY_COLS else SLOTS
    held = nvec + 2 * rank

    def tree(*refs):
        tree_kernel(shape, levels, *refs)

    ortho, child_new, top_new, lowers, window, table = pl.pallas_call(
        tree,
        name="tree",
        out_shape=(
            jax.ShapeDtypeStruct(leaf_basis.shape, F32),
            jax.ShapeDtypeStruct((leaf_count,) + square, F32),
            jax.ShapeDtypeStruct((levels,) + square, F32),
            jax.ShapeDtypeStruct((leaf_count + 1,) + square, F32),
            jax.ShapeDtypeStruct((2,) + vectors.shape, BF16),
            jax.ShapeDtypeStruct((slots, rank, held), BF16),
        ),
        in_specs=[vmem, vmem, vmem, hbm],
        out_specs=(vmem, vmem, vmem, vmem, hbm, hbm),
        scratch_shapes=[
            pltpu.VMEM(vectors.shape, BF16),
            pltpu.VMEM((4, rank, held), BF16),
            pltpu.VMEM((levels,) + square, F32),
            pltpu.VMEM((levels,) + square, F32),
            pltpu.SemaphoreType.DMA,
            pltpu.SemaphoreType.DMA((copies,)),
            pltpu.SemaphoreType.DMA((copies,)),
        ],
        compiler_params=pltpu.CompilerParams(
            collective_id=0, has_side_effects=True, vmem_limit_bytes=32 * 1024 * 1024
        ),
    )(
        leaf_basis,
        child_transfer.reshape((leaf_count,) + square),
        top_transfer.reshape((levels,) + square),
        vectors,
    )

    def apply(*refs):
        apply_kernel(shape, *refs)

    coupling_new, product = pl.pallas_call(
        apply,
        name="apply",
        out_shape=(
            jax.ShapeDtypeStruct((coupling.shape[0],) + square, F32),
            jax.ShapeDtypeStruct(vectors.shape, BF16),
        ),
        in_specs=[vmem] * 8 + [smem] * 6,
        out_specs=(vmem, vmem),
        scratch_shapes=[
            pltpu.VMEM((leaf_count * points, 3 * leaf_count * points), BF16),
            pltpu.VMEM((leaf_count + 1, rank, nvec), F32),
            pltpu.VMEM((leaf_count, rank, nvec), BF16),
        ],
        compiler_params=pltpu.CompilerParams(vmem_limit_bytes=48 * 1024 * 1024),
    )(
        near_blocks,
        window,
        vectors,
        ortho,
        child_new,
        lowers,
        table,
        coupling.reshape((-1,) + square),
        near_rows,
        near_cols,
        near_counts,
        coupling_rows,
        coupling_cols,
        block_counts,
    )
    return (
        ortho,
        child_new.reshape(leaf_count, -1),
        top_new.reshape(1, levels, -1),
        coupling_new.reshape(coupling.shape),
        product,
    )


def solution(mesh):
    shape = (mesh.shape["row"], mesh.shape["col"])
    ranks = (3, 2, 3, 2, 3, 1, 1, 1, 2, 1, 1, 2)

    def run(*args):
        return body(shape, *args)

    def spec(rank):
        return P(AXES, *([None] * (rank - 1)))

    return jax.shard_map(
        run,
        mesh=mesh,
        in_specs=tuple(spec(rank) for rank in ranks),
        out_specs=tuple(spec(rank) for rank in (3, 2, 3, 2, 2)),
        check_vma=False,
    )
```

```python
import jax
import jax.numpy as jnp
from jax import lax
from jax.experimental import pallas as pl
from jax.experimental.pallas import tpu as pltpu
from jax.sharding import PartitionSpec as P

AXES = ("row", "col")
HI = lax.Precision.HIGHEST
F32 = jnp.float32
BF16 = jnp.bfloat16
MESH = pl.DeviceIdType.MESH
PANEL = 8
SENDS = (
    (2, 1, 2, 2),
    (-2, 1, 2, 4),
    (3, 2, 2, 6),
    (-3, 0, 2, 8),
    (1, 1, 1, 0),
    (-1, 2, 1, 1),
    (5, 0, 1, 12),
    (-5, 0, 1, 13),
    (4, 0, 1, 10),
    (-4, 0, 1, 11),
)
SLOTS = 14
RELAY_COLS = 4
RELAY_SLOTS = 38
RELAY_LEVELS = (0, 1)
LATE_LEVEL = 2
NEEDED = {1: (0, 1), 2: (0, 2), 3: (1, 2), 4: (2, 1), 5: (2, 1)}
NEEDED_BACK = {1: (1, 1), 2: (0, 2), 3: (0, 3), 4: (2, 1), 5: (2, 1)}


def mm(a, b, ca=1, cb=0, precision=HI):
    return lax.dot_general(
        a, b, (((ca,), (cb,)), ((), ())), precision=precision, preferred_element_type=F32
    )


def to_squares(flat, squares):
    rank = squares.shape[-1]
    for r in range(rank):
        squares[:, r, :] = flat[:, r * rank : (r + 1) * rank]


def to_rows(squares, flat):
    rank = squares.shape[-1]
    for r in range(rank):
        flat[:, r * rank : (r + 1) * rank] = squares[:, r, :]


def factor(grams):
    n = grams[0].shape[0]
    row = lax.broadcasted_iota(jnp.int32, (n, n), 0)
    col = lax.broadcasted_iota(jnp.int32, (n, n), 1)
    eye = jnp.where(row == col, 1.0, 0.0).astype(F32)
    wide = 2 * n
    top_row = lax.broadcasted_iota(jnp.int32, (PANEL, wide), 0)
    rest_row = lax.broadcasted_iota(jnp.int32, (n - PANEL, wide), 0) + PANEL
    start = tuple(jnp.concatenate([g, eye], axis=1) for g in grams)

    def panel(p, mats):
        live = rest_row < n - PANEL * p
        out = []
        for m in mats:
            top, rest = m[:PANEL], m[PANEL:]
            ctop = [jnp.broadcast_to(top[:, k : k + 1], (PANEL, wide)) for k in range(PANEL)]
            crest = [jnp.broadcast_to(rest[:, k : k + 1], (n - PANEL, wide)) for k in range(PANEL)]
            for j in range(PANEL):
                r = lax.rsqrt(ctop[j][j : j + 1])
                nj = top[j : j + 1] * r
                lt = ctop[j] * r
                lr = jnp.where(live, crest[j] * r, 0.0)
                top = jnp.where(
                    top_row > j, top - lt * nj, jnp.where(top_row == j, nj, top)
                )
                rest = rest - lr * nj
                for k in range(j + 1, PANEL):
                    lk = lt[k : k + 1]
                    ctop[k] = ctop[k] - lt * lk
                    crest[k] = crest[k] - lr * lk
            out.append(pltpu.roll(jnp.concatenate([rest, top], axis=0), wide - PANEL, 1))
        return tuple(out)

    done = lax.fori_loop(0, n // PANEL, panel, start)
    return [(jnp.where(col >= row, m[:, n:], 0.0), m[:, :n]) for m in done]


def tree_kernel(
    shape,
    levels,
    basis_ref,
    child_rows,
    upper_rows,
    vec_ref,
    ortho_ref,
    child_new_ref,
    child_out,
    top_out,
    lower_ref,
    window_ref,
    table_ref,
    x_ref,
    stack_ref,
    term_ref,
    got_ref,
    child_ref,
    upper_ref,
    top_new_ref,
    x_sem,
    send_sem,
    recv_sem,
):
    rows, cols = shape
    total = rows * cols
    me = lax.axis_index("row") * cols + lax.axis_index("col")

    def place(distance):
        other = lax.rem(me + distance + total, total)
        return (other // cols, lax.rem(other, cols))

    def partner(level):
        step = 2**level
        other = me + step * (1 - 2 * lax.rem(me // step, 2))
        return (other // cols, lax.rem(other, cols))

    relay = cols == RELAY_COLS
    here, z = me // cols, lax.rem(me, cols)

    def beside(rows_off, cols_off):
        return (lax.rem(here + rows_off + rows, rows), lax.rem(z + cols_off + cols, cols))

    load = pltpu.make_async_copy(vec_ref, x_ref, x_sem)
    load.start()
    barrier = pltpu.get_barrier_semaphore()
    if relay:
        peers = [place(1), place(-1)]
        peers += [beside(0, 1), beside(0, -1)]
        peers += [beside(1, 0), beside(-1, 0), beside(2, 0), beside(-2, 0)]
    else:
        peers = [place(send[0]) for send in SENDS]
    peers += [partner(level) for level in range(levels)]
    for peer in peers:
        pl.semaphore_signal(barrier, inc=1, device_id=peer, device_id_type=MESH)
    pl.semaphore_wait(barrier, len(peers))

    def remote(at, src, dst, where):
        return pltpu.make_async_remote_copy(
            src_ref=src,
            dst_ref=dst,
            send_sem=send_sem.at[at],
            recv_sem=recv_sem.at[at],
            device_id=where,
            device_id_type=MESH,
        )

    leaf_count, rank, points = basis_ref.shape
    nvec = x_ref.shape[1]
    half = vec_ref.shape[0] // 2

    def vector_copy(part, side):
        at = pl.ds(part * half, half)
        return remote(
            2 * part + side, vec_ref.at[at], window_ref.at[side, at], place(1 - 2 * side)
        )

    vector_copies = [vector_copy(part, side) for part in range(2) for side in range(2)]
    vector_copies[0].start()
    vector_copies[1].start()

    def direct_copy(index):
        distance, first, count, slot = SENDS[index]
        return remote(
            4 + index,
            stack_ref.at[pl.ds(first, count)],
            table_ref.at[pl.ds(slot, count)],
            place(distance),
        )

    def own_row(source, first=0, count=3):
        return table_ref.at[pl.ds((cols + source) * 3 + first, count)]

    def hop(stage, side):
        way = 1 - 2 * side
        at = own_row(z - way * stage)
        return remote(4 + 2 * stage + side, at, at, beside(0, way))

    def hop_in(stage, side):
        way = 1 - 2 * side
        at = own_row(z - way * (stage + 1))
        return remote(4 + 2 * stage + side, at, at, beside(0, way))

    def sends_hop(stage, side):
        if side == 0:
            return jnp.logical_and(z >= stage, z < cols - 1)
        return jnp.logical_and(z < cols - stage, z > 0)

    def gets_hop(stage, side):
        return z > stage if side == 0 else z < cols - 1 - stage

    def row_copies(column, source):
        found = []
        ahead, back = cols + column - source, cols - column + source
        if ahead in NEEDED:
            first, count = NEEDED[ahead]
            found.append(
                remote(
                    10 + source,
                    own_row(source, first, count),
                    table_ref.at[pl.ds(source * 3 + first, count)],
                    beside(1, 0),
                )
            )
        if back in NEEDED_BACK:
            first, count = NEEDED_BACK[back]
            found.append(
                remote(
                    14 + source,
                    own_row(source, first, count),
                    table_ref.at[pl.ds((2 * cols + source) * 3 + first, count)],
                    beside(-1, 0),
                )
            )
        if column == 0 and source == cols - 1:
            found.append(
                remote(
                    18, own_row(source, 2, 1), table_ref.at[pl.ds(9 * cols, 1)], beside(2, 0)
                )
            )
        if column == cols - 1 and source == 0:
            found.append(
                remote(
                    19, own_row(source, 2, 1), table_ref.at[pl.ds(9 * cols + 1, 1)], beside(-2, 0)
                )
            )
        return found

    def start_rows(away):
        for column in range(cols):
            sources = sorted({column - away, column + away})

            @pl.when(z == column)
            def _():
                for source in sources:
                    if 0 <= source < cols:
                        for copy in row_copies(column, source):
                            copy.start()

    def start_hops(stage):
        for side in range(2):

            @pl.when(sends_hop(stage, side))
            def _():
                hop(stage, side).start()

    def take_hops(stage):
        for side in range(2):

            @pl.when(gets_hop(stage, side))
            def _():
                hop_in(stage, side).wait_recv()

    to_squares(child_rows, child_ref)
    to_squares(upper_rows.at[0], upper_ref)
    pad = jnp.zeros((rank, rank), BF16)

    def pack(entry, coeff, lower_t):
        stack_ref[entry, :, :nvec] = coeff.astype(BF16)
        stack_ref[entry, :, nvec:] = jnp.concatenate([lower_t.astype(BF16), pad], axis=1)

    leaves = factor([mm(basis_ref[l], basis_ref[l], 1, 1) for l in range(leaf_count)])
    ortho = [mm(leaves[l][1], basis_ref[l]) for l in range(leaf_count)]
    lifted = [mm(leaves[l][0], child_ref[l]) for l in range(leaf_count)]
    node_gram = mm(lifted[0], lifted[0], 0, 0) + mm(lifted[1], lifted[1], 0, 0)
    for l in range(leaf_count):
        ortho_ref[l] = ortho[l]
        lower_ref[l] = leaves[l][0]
    load.wait()
    coeffs = []
    for l in range(leaf_count):
        coeff = mm(
            ortho[l].astype(BF16), x_ref[l * points : (l + 1) * points, :], precision=None
        )
        coeffs.append(coeff)
        pack(1 + l, coeff, leaves[l][0])
    ((lower_t, inverse),) = factor([node_gram])
    lower_ref[leaf_count] = lower_t
    fresh = [mm(lifted[l], inverse, 1, 1) for l in range(leaf_count)]
    for l in range(leaf_count):
        child_new_ref[l] = fresh[l]
    node_coeff = mm(fresh[0], coeffs[0], 0, 0) + mm(fresh[1], coeffs[1], 0, 0)
    pack(0, node_coeff, lower_t)
    pack(3, node_coeff, lower_t)
    if relay:
        keep = pltpu.make_async_copy(stack_ref.at[pl.ds(1, 3)], own_row(z), x_sem)
        keep.start()
        keep.wait()
        start_hops(0)
        start_rows(0)
    else:
        for index in range(len(SENDS)):
            direct_copy(index).start()
    exchanges = []
    for level in range(levels):
        up = mm(lower_t, upper_ref[level])
        term = mm(up, up, 0, 0)
        term_ref[level] = term
        copy = remote(20 + level, term_ref.at[level], got_ref.at[level], partner(level))
        copy.start()
        exchanges.append(copy)
        if relay and level in RELAY_LEVELS:
            stage = RELAY_LEVELS.index(level)
            take_hops(stage)
            start_hops(stage + 1)
            start_rows(stage + 1)
        if level == LATE_LEVEL:
            vector_copies[2].start()
            vector_copies[3].start()
        copy.wait_recv()
        ((lower_t, inverse),) = factor([term + got_ref[level]])
        top_new_ref[level] = mm(up, inverse, 1, 1)
    to_rows(child_new_ref, child_out)
    to_rows(top_new_ref, top_out.at[0])
    if relay:
        for stage in range(cols - 1):
            if stage >= len(RELAY_LEVELS):
                take_hops(stage)
                if stage + 1 < cols - 1:
                    start_hops(stage + 1)
                start_rows(stage + 1)
        for stage in range(cols - 1):
            for side in range(2):

                @pl.when(sends_hop(stage, side))
                def _():
                    hop(stage, side).wait_send()

        for column in range(cols):

            @pl.when(z == column)
            def _():
                for source in range(cols):
                    for copy in row_copies(column, source):
                        copy.wait_send()
                for source in range(cols):
                    for copy in row_copies(column, source):
                        copy.wait_recv()

    else:
        for index in range(len(SENDS)):
            direct_copy(index).wait()
    for copy in exchanges:
        copy.wait_send()
    for copy in vector_copies:
        copy.wait()


def apply_kernel(
    shape,
    blocks_ref,
    window_ref,
    vec_ref,
    ortho_ref,
    child_ref,
    lower_ref,
    table_ref,
    coupling_rows_ref,
    near_rows,
    near_cols,
    near_counts,
    far_rows,
    far_cols,
    far_counts,
    coupling_out,
    product_ref,
    near_ref,
    far_ref,
    desc_ref,
    coupling_ref,
    coupling_new_ref,
):
    to_squares(coupling_rows_ref, coupling_ref)
    me = lax.axis_index("row") * shape[1] + lax.axis_index("col")
    slots, points, _ = blocks_ref.shape
    leaf_count, rank, _ = ortho_ref.shape
    nvec = vec_ref.shape[1]
    reach = window_ref.shape[1] // points
    near_ref[...] = jnp.zeros_like(near_ref)
    for b in range(slots):

        @pl.when(b < near_counts[0])
        def _():
            r = near_rows[b] - me * leaf_count
            c = near_cols[b] - me * leaf_count + reach
            near_ref[
                pl.ds(pl.multiple_of(r * points, points), points),
                pl.ds(pl.multiple_of(c * points, points), points),
            ] = blocks_ref[b]

    far_ref[...] = jnp.zeros_like(far_ref)
    split = coupling_ref.shape[0] * leaf_count // (leaf_count + 1)
    for b in range(coupling_ref.shape[0]):
        upper = b >= split
        if upper:
            active = b - split < far_counts[0, 1]
            row = leaf_count
            delta = far_cols[b] - me
            slot = jnp.where(
                delta == -3,
                7,
                jnp.where(
                    delta == 3,
                    8,
                    jnp.where(
                        delta == -4, 10, jnp.where(delta == 4, 11, jnp.where(delta == -5, 12, 13))
                    ),
                ),
            )
        else:
            active = b < far_counts[0, 0]
            row = jnp.where(active, far_rows[b] - me * leaf_count, 0)
            delta = far_cols[b] - me * leaf_count
            odd = lax.rem(far_cols[b], 2)
            slot = jnp.where(
                delta < -4,
                6,
                jnp.where(
                    delta < -2,
                    2 + odd,
                    jnp.where(
                        delta < 0, 0, jnp.where(delta < 4, 1, jnp.where(delta < 6, 4 + odd, 9))
                    ),
                ),
            )
        if shape[1] == RELAY_COLS:
            cols = shape[1]
            span = 1 if upper else leaf_count
            entry = leaf_count if upper else lax.rem(far_cols[b], leaf_count)
            source = jnp.where(active, far_cols[b] // span, me)
            apart = source // cols - me // cols
            slot = ((apart + 1) * cols + lax.rem(source, cols)) * 3 + entry
            slot = jnp.where(apart < -1, 9 * cols, jnp.where(apart > 1, 9 * cols + 1, slot))
        else:
            slot = jnp.where(active, slot, 0)
        item = table_ref[slot]
        half = mm(lower_ref[row], coupling_ref[b])
        new = mm(half, item[:, nvec : nvec + rank].astype(F32), 1, 1)
        new = jnp.where(active, new, 0.0)
        coupling_new_ref[b] = new
        low = new.astype(BF16)
        term = mm(low, item[:, :nvec], precision=None)
        far_ref[row] = far_ref[row] + term
    to_rows(coupling_new_ref, coupling_out)
    for l in range(leaf_count):
        desc_ref[l] = (far_ref[l] + mm(child_ref[l], far_ref[leaf_count])).astype(BF16)
    tile = 256

    @pl.loop(0, nvec // tile)
    def _(step):
        at = pl.ds(pl.multiple_of(step * tile, tile), tile)
        side = reach * points
        acc = mm(near_ref[:, :side], window_ref[0, :, at], precision=None)
        acc = acc + mm(
            near_ref[:, side : side + leaf_count * points], vec_ref[:, at], precision=None
        )
        acc = acc + mm(
            near_ref[:, side + leaf_count * points :], window_ref[1, :, at], precision=None
        )
        for l in range(leaf_count):
            far = mm(ortho_ref[l].astype(BF16), desc_ref[l, :, at], 0, 0, precision=None)
            product_ref[l * points : (l + 1) * points, at] = (
                acc[l * points : (l + 1) * points] + far
            ).astype(BF16)


def body(
    shape,
    leaf_basis,
    child_transfer,
    top_transfer,
    vectors,
    near_blocks,
    near_rows,
    near_cols,
    near_counts,
    coupling,
    coupling_rows,
    coupling_cols,
    block_counts,
):
    leaf_count, rank, points = leaf_basis.shape
    nvec = vectors.shape[1]
    levels = top_transfer.shape[1]
    square = (rank, rank)
    vmem = pl.BlockSpec(memory_space=pltpu.VMEM)
    smem = pl.BlockSpec(memory_space=pltpu.SMEM)
    hbm = pl.BlockSpec(memory_space=pl.ANY)
    copies = 20 + levels
    slots = RELAY_SLOTS if shape[1] == RELAY_COLS else SLOTS
    held = nvec + 2 * rank

    def tree(*refs):
        tree_kernel(shape, levels, *refs)

    ortho, child_new, child_out, top_out, lowers, window, table = pl.pallas_call(
        tree,
        name="tree",
        out_shape=(
            jax.ShapeDtypeStruct(leaf_basis.shape, F32),
            jax.ShapeDtypeStruct((leaf_count,) + square, F32),
            jax.ShapeDtypeStruct(child_transfer.shape, F32),
            jax.ShapeDtypeStruct(top_transfer.shape, F32),
            jax.ShapeDtypeStruct((leaf_count + 1,) + square, F32),
            jax.ShapeDtypeStruct((2,) + vectors.shape, BF16),
            jax.ShapeDtypeStruct((slots, rank, held), BF16),
        ),
        in_specs=[vmem, vmem, vmem, hbm],
        out_specs=(vmem, vmem, vmem, vmem, vmem, hbm, hbm),
        scratch_shapes=[
            pltpu.VMEM(vectors.shape, BF16),
            pltpu.VMEM((4, rank, held), BF16),
            pltpu.VMEM((levels,) + square, F32),
            pltpu.VMEM((levels,) + square, F32),
            pltpu.VMEM((leaf_count,) + square, F32),
            pltpu.VMEM((levels,) + square, F32),
            pltpu.VMEM((levels,) + square, F32),
            pltpu.SemaphoreType.DMA,
            pltpu.SemaphoreType.DMA((copies,)),
            pltpu.SemaphoreType.DMA((copies,)),
        ],
        compiler_params=pltpu.CompilerParams(
            collective_id=0, has_side_effects=True, vmem_limit_bytes=60 * 1024 * 1024
        ),
    )(
        leaf_basis,
        child_transfer,
        top_transfer,
        vectors,
    )

    def apply(*refs):
        apply_kernel(shape, *refs)

    coupling_new, product = pl.pallas_call(
        apply,
        name="apply",
        out_shape=(
            jax.ShapeDtypeStruct(coupling.shape, F32),
            jax.ShapeDtypeStruct(vectors.shape, BF16),
        ),
        in_specs=[vmem] * 8 + [smem] * 6,
        out_specs=(vmem, vmem),
        scratch_shapes=[
            pltpu.VMEM((leaf_count * points, 3 * leaf_count * points), BF16),
            pltpu.VMEM((leaf_count + 1, rank, nvec), F32),
            pltpu.VMEM((leaf_count, rank, nvec), BF16),
            pltpu.VMEM((coupling.shape[0],) + square, F32),
            pltpu.VMEM((coupling.shape[0],) + square, F32),
        ],
        compiler_params=pltpu.CompilerParams(vmem_limit_bytes=60 * 1024 * 1024),
    )(
        near_blocks,
        window,
        vectors,
        ortho,
        child_new,
        lowers,
        table,
        coupling,
        near_rows,
        near_cols,
        near_counts,
        coupling_rows,
        coupling_cols,
        block_counts,
    )
    return (
        ortho,
        child_out,
        top_out,
        coupling_new,
        product,
    )


def solution(mesh):
    shape = (mesh.shape["row"], mesh.shape["col"])
    ranks = (3, 2, 3, 2, 3, 1, 1, 1, 2, 1, 1, 2)

    def run(*args):
        return body(shape, *args)

    def spec(rank):
        return P(AXES, *([None] * (rank - 1)))

    return jax.shard_map(
        run,
        mesh=mesh,
        in_specs=tuple(spec(rank) for rank in ranks),
        out_specs=tuple(spec(rank) for rank in (3, 2, 3, 2, 2)),
        check_vma=False,
    )
```
